256 devices in a mesh: dp: 16 (over x, z_hi), ctx: 16 (over z_lo, y, core).
Axes of the slice: x: 4, y: 4, z: 8 (z_hi: 4, z_lo: 2; z = z_hi * 2 + z_lo), core: 2. Of those that a mesh axis runs over, the one named last changes fastest.
Arguments:
- hidden_in: bfloat16 [16, 4096, 8192], P('dp', 'ctx'), may hold values from -6 to 6
- queries: bfloat16 [16, 4096, 4096], P('dp', 'ctx'), may hold values from -128 to 128
- key_projection_weight: bfloat16 [8192, 512], P('dp'), may hold values from -0.0625 to 0.0625
- value_projection_weight: bfloat16 [8192, 512], P('dp'), may hold values from -0.0625 to 0.0625
- key_projection_bias: float32 [512], replicated, may hold values from -2.5 to 2.5
- value_projection_bias: float32 [512], replicated, may hold values from -3 to 3
- block_segments: int32 [16, 32], P('dp'), may hold values from 0 to 4, never falling along the last dimension, each value on 1 to 12 neighbouring positions
Outputs:
- attended: bfloat16 [16, 4096, 4096], P('dp', 'ctx')
The draws below stay inside these ranges and needn't reach their ends.
Inputs may be any that keep to these rules, and one draw needn't show every extreme that they name: `block_segments`: each row starts with segment 0 and never falls; every one of the 5 segments spans 1 to 12 blocks.
All inputs are finite; a program needn't handle non-finite values.
Results may differ from the reference program's by a relative error of at most 0.0079.
Values may be sent and summed in bfloat16 or wider, within the bound.
A program may use at most 128 MiB of HBM per device.

```python
import math
import jax
import jax.numpy as jnp
import numpy as np
from jax import lax

MODEL_WIDTH = 8192
HEAD_SIZE = 128
QUERY_HEADS = 32
KEY_VALUE_HEADS = 4
BLK = 128
SEGS = 5
PACK_LENGTH = 4096
NBLK = 32
MOST = 12
PACKS = 16


def key_bias_entries(key):
    random_subkey = jax.random.fold_in(key, 17)
    unscaled_sample = jax.random.normal(random_subkey, (KEY_VALUE_HEADS * HEAD_SIZE,), jnp.float32)
    return 0.5 * jnp.clip(unscaled_sample, -3.0, 3.0)


def draw_key_projection_bias(key, part):
    return key_bias_entries(key)


def draw_queries(key, part):
    base_key = jax.random.fold_in(key, 23)
    shape_all = (PACKS, PACK_LENGTH, QUERY_HEADS * HEAD_SIZE)
    return jnp.clip(jax.random.normal(base_key, shape_all, jnp.float32), -6.0, 6.0).astype(jnp.bfloat16)


def shard_levels(own_key, shape, split, least, high):
    level, own = 1.0, jax.random.fold_in(own_key, 6)
    for axis_at, shards_of in split:
        heights = jnp.exp(jax.random.uniform(jax.random.fold_in(own, axis_at), (shards_of,), jnp.float32, least / len(split), high / len(split)))
        level = level * jnp.repeat(heights, shape[axis_at] // shards_of).reshape([-1 if axis == axis_at else 1 for axis in range(len(shape))])
    return level


def profile(number_of, total, bound, slope):
    weights = [(1 << 20) // math.isqrt(rank ** slope) + 1 for rank in range(2, number_of + 1)]
    rest, holding = total - bound - (number_of - 1), [1] * (number_of - 1)
    while rest > 0:
        free = [i for i in range(number_of - 1) if holding[i] < bound]
        mass, left = sum([weights[i] for i in free]), rest
        for i in free:
            more = min(bound - holding[i], max(1, left * weights[i] // mass), rest)
            holding[i] = holding[i] + more
            rest = rest - more
    return np.array([bound] + holding)


def uneven_parts(stream_key, number_of, total, limit, skew):
    if number_of == 2:
        one = jax.random.randint(stream_key, (), max(1, total - limit), min(limit, total - 1) + 1)
        return jnp.stack([one, total - one])
    tallies = jnp.asarray(profile(number_of, total, limit, skew), jnp.int32)
    pairs = (number_of - 1) // 2
    source_of, receiver = tallies[1:1 + 2 * pairs:2], tallies[2:2 + 2 * pairs:2]
    margin = jnp.minimum(source_of - 1, limit - receiver)
    moved = jax.random.randint(jax.random.fold_in(stream_key, 1), (pairs,), 0, 1 << 20) % (margin + 1)
    tallies = tallies.at[1:1 + 2 * pairs:2].set(source_of - moved).at[2:2 + 2 * pairs:2].set(receiver + moved)
    return tallies[jax.random.permutation(jax.random.fold_in(stream_key, 2), number_of)]


def bell_draw(rng, extent, scale, limit, split=(), held_as=jnp.bfloat16):
    drawn = scale * jax.random.normal(rng, extent, jnp.float32)
    if split:
        drawn = drawn * shard_levels(rng, extent, split, -0.22, 0.18)
    return jnp.clip(drawn, -limit, limit).astype(held_as)


def setup_inputs(seed: int = 0) -> dict:
    splits = jax.random.split(jax.random.key(seed), 8)
    hidden_in = bell_draw(splits[0], (PACKS, PACK_LENGTH, MODEL_WIDTH), 1.0, 6.0, ((0, 16), (1, 16)))
    queries = draw_queries(jax.random.fold_in(splits[7], 71), 0)
    key_projection_weight = bell_draw(splits[2], (MODEL_WIDTH, KEY_VALUE_HEADS * HEAD_SIZE), MODEL_WIDTH ** -0.5, 0.0625, ((0, 16),))
    value_projection_weight = bell_draw(splits[3], (MODEL_WIDTH, KEY_VALUE_HEADS * HEAD_SIZE), MODEL_WIDTH ** -0.5, 0.0625, ((0, 16),))
    key_projection_bias = draw_key_projection_bias(jax.random.fold_in(splits[7], 71), 0)
    value_projection_bias = bell_draw(splits[5], (KEY_VALUE_HEADS * HEAD_SIZE,), 0.5, 3.0, (), jnp.float32)
    block_segments = jax.vmap(lambda own: jnp.searchsorted(jnp.cumsum(uneven_parts(own, SEGS, NBLK, MOST, 0)), jnp.arange(NBLK), side="right"))(jax.random.split(splits[6], PACKS)).reshape((PACKS, NBLK)).astype(jnp.int32)
    return dict(hidden_in=hidden_in, queries=queries, key_projection_weight=key_projection_weight, value_projection_weight=value_projection_weight, key_projection_bias=key_projection_bias, value_projection_bias=value_projection_bias, block_segments=block_segments)


rope_base = 1000000.0

def rotary_rotate(head_vecs, token_positions):
    half_dim = head_vecs.shape[-1] // 2
    frequency = rope_base ** (-(jnp.arange(half_dim, dtype=jnp.float32) * 2.0 / head_vecs.shape[-1]))
    angles = token_positions.astype(jnp.float32)[:, None] * frequency[None, :]
    cos_part = jnp.cos(angles)[:, None, :]
    sine_part = jnp.sin(angles)[:, None, :]
    first_half = head_vecs[..., :half_dim]
    second_half = head_vecs[..., half_dim:]
    return jnp.concatenate([first_half * cos_part - second_half * sine_part, second_half * cos_part + first_half * sine_part], axis=-1)

def reference(hidden_in, queries, key_projection_weight, value_projection_weight, key_projection_bias, value_projection_bias, block_segments):
    group_width = QUERY_HEADS // KEY_VALUE_HEADS
    rows_per_block = math.gcd(PACK_LENGTH, 512)
    block_count = PACK_LENGTH // rows_per_block
    token_positions = jnp.arange(PACK_LENGTH, dtype=jnp.int32)
    score_scale = 1.0 / math.sqrt(HEAD_SIZE)

    def one_pack(packed):
        pack_tokens, packed_query_rows, pack_segs = packed
        key_projected_rows = jnp.dot(pack_tokens, key_projection_weight, preferred_element_type=jnp.float32) + key_projection_bias
        key_row_values = rotary_rotate(key_projected_rows.reshape(PACK_LENGTH, KEY_VALUE_HEADS, HEAD_SIZE), token_positions)
        key_row_values = lax.optimization_barrier(key_row_values.astype(jnp.bfloat16)).astype(jnp.float32)
        value_proj = jnp.dot(pack_tokens, value_projection_weight, preferred_element_type=jnp.float32) + value_projection_bias
        value_row_values = lax.optimization_barrier(value_proj.astype(jnp.bfloat16)).astype(jnp.float32)
        value_row_values = value_row_values.reshape(PACK_LENGTH, KEY_VALUE_HEADS, HEAD_SIZE)
        segment_tokens = jnp.repeat(pack_segs, BLK)

        def single_block(blocked):
            block_queries, block_pos, block_seg = blocked
            scores = jnp.einsum('tkgd,skd->tkgs', block_queries.astype(jnp.float32), key_row_values) * score_scale
            allowed = (token_positions[None, :] <= block_pos[:, None]) & ((segment_tokens[None, :] == block_seg[:, None]) | (segment_tokens[None, :] == 0))
            scores = jnp.where(allowed[:, None, None, :], scores, -jnp.inf)
            row_peak = lax.optimization_barrier(jnp.max(scores, axis=-1, keepdims=True))
            probs = jnp.exp(scores - row_peak)
            row_total = lax.optimization_barrier(jnp.sum(probs, axis=-1))
            rounded = lax.optimization_barrier(probs.astype(jnp.bfloat16)).astype(jnp.float32)
            mixed = jnp.einsum('tkgs,skd->tkgd', rounded, value_row_values) / row_total[..., None]
            return mixed.astype(jnp.bfloat16).reshape(rows_per_block, QUERY_HEADS * HEAD_SIZE)
        output_rows = lax.map(single_block, (packed_query_rows.reshape(block_count, rows_per_block, KEY_VALUE_HEADS, group_width, HEAD_SIZE), token_positions.reshape(block_count, rows_per_block), segment_tokens.reshape(block_count, rows_per_block)))
        return output_rows.reshape(PACK_LENGTH, QUERY_HEADS * HEAD_SIZE)
    return lax.map(one_pack, (hidden_in, queries, block_segments))
```

```python
import functools
import math

import jax
import jax.numpy as jnp
from jax import lax
from jax.experimental import pallas as pl
from jax.experimental.pallas import tpu as pltpu
from jax.sharding import PartitionSpec as P

MESH = pl.DeviceIdType.MESH
D = 128
BLK = 128
ROPE_BASE = 1000000.0
BIG = 1e30
SCALE = math.log2(math.e) / math.sqrt(D)
VMEM_LIMIT = 56 * 1024 * 1024


def rope_tables(first, count):
    half = D // 2
    frequency = ROPE_BASE ** (-(jnp.arange(half, dtype=jnp.float32) * 2.0 / D))
    positions = (first + jnp.arange(count, dtype=jnp.int32)).astype(jnp.float32)
    angles = positions[:, None] * frequency[None, :]
    cos, sin = jnp.cos(angles), jnp.sin(angles)
    return jnp.concatenate([cos, cos], axis=1), jnp.concatenate([-sin, sin], axis=1)


def gather_kernel(
    hid, q, wk, wv, bk, bv, cos, sin, kv_out, q2,
    hbuf, wbuf, acc, kv,
    lsem, hsend, hrecv, wsend, wrecv, ksend, krecv,
):
    dp, ctx = lax.axis_index("dp"), lax.axis_index("ctx")
    x, zh = dp // 4, dp % 4
    zl, y, core = ctx // 8, (ctx // 2) % 4, ctx % 2
    z = 2 * zh + zl
    m = zl * 4 + y

    def zdev(at):
        return (x * 4 + at // 2, (at % 2) * 8 + ctx % 8)

    xp, xm = (((x + 1) % 4) * 4 + zh, ctx), (((x + 3) % 4) * 4 + zh, ctx)
    zp, zm = zdev((z + 1) % 8), zdev((z + 7) % 8)
    yp = (dp, zl * 8 + ((y + 1) % 4) * 2 + core)
    ym = (dp, zl * 8 + ((y + 3) % 4) * 2 + core)
    sib = (dp, ctx + 1 - 2 * core)
    near = (xp, xm, zp, zm, yp, ym, sib)

    def weights_in(g, which):
        head = pl.multiple_of((2 * core + g) * D, D)
        src = (wk, wv)[which].at[:, pl.ds(head, D)]
        return pltpu.make_async_copy(src, wbuf.at[g, dp, :, pl.ds(which * D, D)], lsem.at[2 * g + which])

    def hidden_in(j):
        at = (x + j) % 4
        cols = pl.ds(pl.multiple_of(at * 2048, 2048), 2048)
        rows = pl.ds(pl.multiple_of(core * 256, 256), 256)
        local = pltpu.make_async_copy(hid.at[:, cols], hbuf.at[at, rows], lsem.at[4 + j])
        remote = pltpu.make_async_remote_copy(
            hid.at[:, cols], hbuf.at[at, rows], hsend.at[j], hrecv.at[j], device_id=sib, device_id_type=MESH)
        return local, remote

    def hidden_landed(j):
        at = (x + j) % 4
        cols = pl.ds(pl.multiple_of(at * 2048, 2048), 2048)
        rows = pl.ds(pl.multiple_of((1 - core) * 256, 256), 256)
        return pltpu.make_async_remote_copy(
            hid.at[:, cols], hbuf.at[at, rows], hsend.at[j], hrecv.at[j], device_id=sib, device_id_type=MESH)

    my_rows = pl.ds(pl.multiple_of(core * 256, 256), 256)
    q_local = pltpu.make_async_copy(
        q.at[:, pl.ds(pl.multiple_of(core * 2048, 2048), 2048)], q2.at[my_rows], lsem.at[8])
    q_remote = pltpu.make_async_remote_copy(
        q.at[:, pl.ds(pl.multiple_of((1 - core) * 2048, 2048), 2048)], q2.at[my_rows],
        hsend.at[4], hrecv.at[4], device_id=sib, device_id_type=MESH)

    for g in range(2):
        for which in range(2):
            weights_in(g, which).start()

    barrier = pltpu.get_barrier_semaphore()
    for to in near:
        pl.semaphore_signal(barrier, inc=1, device_id=to, device_id_type=MESH)
    pl.semaphore_wait(barrier, len(near))

    def lane(k):
        j = k - 1
        return j + j // 2 - 2 * (j // 3)

    def row_of(base, kind):
        return base + (128 if kind == 3 else 0), (256 if kind < 2 else 128)

    def piece(g, shard, base, kind):
        start, size = row_of(base, kind)
        return wbuf.at[g, shard, pl.ds(start, size)]

    def copy(ref, to, g, task, kind):
        at = (g * 10 + task) * 4 + kind
        return pltpu.make_async_remote_copy(
            ref, ref, wsend.at[at], wrecv.at[at], device_id=to, device_id_type=MESH)

    def x_at(k):
        return (zh, 0) if isinstance(k, int) and k == 0 else ((zh + lane(k)) % 4, 256)

    def z_at(k):
        return (x, 256) if isinstance(k, int) and k == 0 else ((x + lane(k)) % 4, 0)

    def x_send(g, k, kind):
        at, base = x_at(k)
        shard = ((x + (0, 0, 3, 1)[kind]) % 4) * 4 + at
        copy(piece(g, shard, base, kind), (xp, xm)[kind % 2], g, k, kind).start()

    def x_wait(g, k, kind):
        at, base = x_at(k)
        shard = ((x + (3, 1, 2, 2)[kind]) % 4) * 4 + at
        copy(piece(g, shard, base, kind), xp, g, k, kind).wait_recv()

    def z_send(g, k, kind):
        at, base = z_at(k)
        off = (zl + 3, zl, zl + 2, zl + 1)[kind]
        shard = at * 4 + (zh + off) % 4
        copy(piece(g, shard, base, kind), (zp, zm)[kind % 2], g, k + 5, kind).start()

    def z_wait(g, k, kind):
        at, base = z_at(k)
        shard = at * 4 + (zh + (3, 1, 2, 2)[kind]) % 4
        copy(piece(g, shard, base, kind), zp, g, k + 5, kind).wait_recv()

    def x_start(g, k):
        x_send(g, k, 0)
        x_send(g, k, 1)

    def z_start(g, k):
        @pl.when(zl == 1)
        def _():
            z_send(g, k, 0)

        @pl.when(zl == 0)
        def _():
            z_send(g, k, 1)

    def z_step(g, k, kind):
        z_wait(g, k, kind)
        even, odd = ((0, 2), (3, 1), (2, None), (None, 3))[kind]
        if even is not None:
            @pl.when(zl == 0)
            def _():
                z_send(g, k, even)
        if odd is not None:
            @pl.when(zl == 1)
            def _():
                z_send(g, k, odd)

    def x_step(g, k, kind):
        x_wait(g, k, kind)
        if kind < 2:
            x_send(g, k, kind + 2)

    def begin(g):
        weights_in(g, 0).wait()
        weights_in(g, 1).wait()
        x_start(g, 0)
        z_start(g, 0)
        x_start(g, 1)
        z_start(g, 1)

    def first(g):
        x_step(g, 0, 0)
        z_start(g, 3)
        z_step(g, 0, 0)
        x_start(g, 3)
        x_step(g, 0, 1)
        z_start(g, 2)
        z_step(g, 0, 1)
        x_start(g, 2)
        x_step(g, 0, 2)
        x_step(g, 0, 3)
        z_start(g, 4)
        z_step(g, 0, 2)
        z_step(g, 0, 3)
        x_start(g, 4)

    def later(g, k):
        for kind in range(4):
            x_step(g, k, kind)
            z_step(g, k, kind)

    def product(g, sx, sz, base):
        return jnp.dot(
            hbuf[sx, :, pl.ds(pl.multiple_of(sz * 512 + base, 256), 256)],
            wbuf[g, sx * 4 + sz, pl.ds(base, 256)],
            preferred_element_type=jnp.float32,
        )

    def multiply(g, k):
        at, base = x_at(k)
        total = acc[...]
        for off in (3, 1, 2):
            total += product(g, (x + off) % 4, at, base)
        at, base = z_at(k)
        for off in (3, 1, 2):
            total += product(g, at, (zh + off) % 4, base)
        acc[...] = total

    def own(g):
        acc[...] = product(g, x, zh, 0) + product(g, x, zh, 256)

    def kcopy(g, at, kind, unit, to):
        start, size = (256 if kind == 3 else 0), (512 if kind < 2 else 256)
        ref = kv.at[g, unit, pl.ds(start, size)]
        n = g * 9 + at + kind
        return pltpu.make_async_remote_copy(ref, ref, ksend.at[n], krecv.at[n], device_id=to, device_id_type=MESH)

    def k_send(g, line, kind):
        unit = line * 4 + (y + (0, 0, 3, 1)[kind]) % 4
        at = 4 if isinstance(line, int) else 0
        kcopy(g, at, kind, unit, (yp, ym)[kind % 2]).start()

    def k_wait(g, line, kind):
        unit = line * 4 + (y + (3, 1, 2, 2)[kind]) % 4
        at = 4 if isinstance(line, int) else 0
        kcopy(g, at, kind, unit, yp).wait_recv()

    def cross(g, unit):
        ref = kv.at[g, unit]
        n = g * 9 + 8
        to = (dp, ctx % 8 + 8)
        return pltpu.make_async_remote_copy(ref, ref, ksend.at[n], krecv.at[n], device_id=to, device_id_type=MESH)

    def kv_begin(g):
        total = acc[...]
        head = 2 * core + g
        key = total[:, :D] + bk[head]
        turned = jnp.concatenate([key[:, D // 2:], key[:, : D // 2]], axis=1)
        key = key * cos[...] + turned * sin[...]
        value = total[:, D:] + bv[head]
        kv[g, m] = jnp.concatenate([key, value], axis=1).astype(jnp.bfloat16)

        @pl.when(zl == 0)
        def _():
            cross(g, m).start()
        k_send(g, zl, 0)
        k_send(g, zl, 1)

    def kv_one(g):
        for kind in range(2):
            k_wait(g, zl, kind)
            k_send(g, zl, kind + 2)

        @pl.when(zl == 1)
        def _():
            cross(g, y).wait_recv()
            k_send(g, 0, 0)
            k_send(g, 0, 1)

    def kv_two(g):
        k_wait(g, zl, 2)
        k_wait(g, zl, 3)

        @pl.when(zl == 1)
        def _():
            for kind in range(2):
                k_wait(g, 0, kind)
                k_send(g, 0, kind + 2)

    def kv_three(g):
        @pl.when(zl == 1)
        def _():
            k_wait(g, 0, 2)
            k_wait(g, 0, 3)

    def kv_leave(g):
        return pltpu.make_async_copy(kv.at[g], kv_out.at[g], lsem.at[9 + g])

    def kv_sent(g):
        for kind in range(4):
            kcopy(g, 0, kind, m, yp).wait_send()

        @pl.when(zl == 1)
        def _():
            for kind in range(4):
                kcopy(g, 4, kind, m, yp).wait_send()

        @pl.when(zl == 0)
        def _():
            cross(g, m).wait_send()

    begin(0)
    for j in (0, 1, 3, 2):
        local, remote = hidden_in(j)
        local.start()
        remote.start()
    q_local.start()
    q_remote.start()
    first(0)
    later(0, 1)
    for j in (0, 1, 3, 2):
        hidden_in(j)[0].wait()
        hidden_landed(j).wait_recv()
    own(0)
    multiply(0, 0)
    multiply(0, 1)

    def step0(k, carry):
        later(0, k)
        multiply(0, k)
        return carry

    lax.fori_loop(2, 4, step0, 0)
    begin(1)
    later(0, 4)
    multiply(0, 4)
    kv_begin(0)
    first(1)
    own(1)
    multiply(1, 0)
    kv_one(0)
    later(1, 1)
    multiply(1, 1)
    kv_two(0)
    later(1, 2)
    multiply(1, 2)
    kv_three(0)

    kv_leave(0).start()

    def step1(k, carry):
        later(1, k)
        multiply(1, k)
        return carry

    lax.fori_loop(3, 5, step1, 0)
    kv_begin(1)
    kv_one(1)
    kv_two(1)
    kv_three(1)
    kv_leave(1).start()

    def drain(task, carry):
        for kind in range(4):
            start, size = row_of(0, kind)
            ref = wbuf.at[0, 0, pl.ds(start, size)]
            at = task * 4 + kind
            pltpu.make_async_remote_copy(
                ref, ref, wsend.at[at], wrecv.at[at], device_id=xp, device_id_type=MESH).wait_send()
        return carry

    lax.fori_loop(0, 20, drain, 0)
    for g in range(2):
        kv_sent(g)
    for j in range(4):
        hidden_in(j)[1].wait_send()
    q_local.wait()
    q_remote.wait_send()
    other = pl.ds(pl.multiple_of((1 - core) * 256, 256), 256)
    pltpu.make_async_remote_copy(
        q.at[:, pl.ds(0, 2048)], q2.at[other], hsend.at[4], hrecv.at[4], device_id=sib, device_id_type=MESH).wait_recv()
    kv_leave(0).wait()
    kv_leave(1).wait()


def gathered(hid, q, wk, wv, bk, bv, cos, sin):
    vmem, anywhere = pl.BlockSpec(memory_space=pltpu.VMEM), pl.BlockSpec(memory_space=pl.ANY)
    bf16 = jnp.bfloat16
    return pl.pallas_call(
        gather_kernel,
        out_shape=(jax.ShapeDtypeStruct((2, 8, 512, 256), bf16), jax.ShapeDtypeStruct((512, 2048), bf16)),
        in_specs=[anywhere] * 4 + [vmem] * 4,
        out_specs=(anywhere, anywhere),
        scratch_shapes=[
            pltpu.VMEM((4, 512, 2048), bf16),
            pltpu.VMEM((2, 16, 512, 256), bf16),
            pltpu.VMEM((512, 256), jnp.float32),
            pltpu.VMEM((2, 8, 512, 256), bf16),
            pltpu.SemaphoreType.DMA((11,)),
            pltpu.SemaphoreType.DMA((5,)),
            pltpu.SemaphoreType.DMA((5,)),
            pltpu.SemaphoreType.DMA((80,)),
            pltpu.SemaphoreType.DMA((80,)),
            pltpu.SemaphoreType.DMA((18,)),
            pltpu.SemaphoreType.DMA((18,)),
        ],
        compiler_params=pltpu.CompilerParams(
            collective_id=0, has_side_effects=True, vmem_limit_bytes=VMEM_LIMIT),
        name="gather",
    )(hid, q, wk, wv, bk, bv, cos, sin)


def attend_kernel(segs, place, q, kv, out, scores, peak, total, acc):
    b = pl.program_id(1)
    t = place[0] + b
    mine = segs[t]

    def count(i, carry):
        before = (i < t).astype(jnp.int32)
        premise = (segs[i] == 0).astype(jnp.int32)
        same = (segs[i] == mine).astype(jnp.int32)
        return (carry[0] + before * premise, carry[1] + before * (1 - premise) * same)

    p, o = lax.fori_loop(0, 32, count, (jnp.int32(0), jnp.int32(0)))
    n = p + o
    full = n // 2

    def slot(j):
        return pl.multiple_of(jnp.where(j < p, j, j - p + t - o) * BLK, BLK)

    peak[...] = jnp.full_like(peak, -BIG)

    def score(c, first, second, mask):
        keys = jnp.concatenate([kv[0, pl.ds(first, BLK), :D], kv[0, pl.ds(second, BLK), :D]], axis=0)
        for j in range(8):
            rows = pl.ds(j * BLK, BLK)
            s = lax.dot_general(
                q[:, j * D:(j + 1) * D], keys, (((1,), (1,)), ((), ())), preferred_element_type=jnp.float32) * SCALE
            if mask is not None:
                s = jnp.where(mask, s, -BIG)
            scores[c, rows] = s
            peak[rows] = jnp.maximum(peak[rows], jnp.maximum(s[:, :BLK], s[:, BLK:]))

    def one(c, carry):
        score(c, slot(2 * c), slot(2 * c + 1), None)
        return carry

    lax.fori_loop(0, full, one, 0)
    odd = n % 2
    extra, diagonal = slot(jnp.maximum(n - 1, 0)), pl.multiple_of(t * BLK, BLK)
    row = lax.broadcasted_iota(jnp.int32, (BLK, 2 * BLK), 0)
    col = lax.broadcasted_iota(jnp.int32, (BLK, 2 * BLK), 1)
    least = jnp.where(col < BLK, jnp.where(odd == 1, -1, BLK), col - BLK)
    score(full, extra, diagonal, row >= least)

    peak[...] = jnp.broadcast_to(jnp.max(peak[...], axis=1, keepdims=True), peak.shape)
    total[...] = jnp.zeros_like(total)
    acc[...] = jnp.zeros_like(acc)

    def weigh(c, first, second):
        values = jnp.concatenate([kv[0, pl.ds(first, BLK), D:], kv[0, pl.ds(second, BLK), D:]], axis=0)
        for j in range(8):
            rows = pl.ds(j * BLK, BLK)
            top = peak[rows]
            left = jnp.exp2(scores[c, rows, :BLK] - top)
            right = jnp.exp2(scores[c, rows, BLK:] - top)
            total[rows] += left + right
            weights = jnp.concatenate([left, right], axis=1).astype(jnp.bfloat16)
            acc[rows] += jnp.dot(weights, values, preferred_element_type=jnp.float32)

    def two(c, carry):
        weigh(c, slot(2 * c), slot(2 * c + 1))
        return carry

    lax.fori_loop(0, full, two, 0)
    weigh(full, extra, diagonal)
    for j in range(8):
        rows = pl.ds(j * BLK, BLK)
        out[:, j * D:(j + 1) * D] = (acc[rows] / jnp.sum(total[rows], axis=1, keepdims=True)).astype(jnp.bfloat16)


def attended(segs, place, q2, kv):
    return pl.pallas_call(
        attend_kernel,
        out_shape=jax.ShapeDtypeStruct((512, 2048), jnp.bfloat16),
        grid_spec=pltpu.PrefetchScalarGridSpec(
            num_scalar_prefetch=2,
            grid=(2, 4),
            in_specs=[
                pl.BlockSpec((BLK, 8 * D), lambda g, b, *_: (b, g)),
                pl.BlockSpec((1, 4096, 2 * D), lambda g, b, *_: (g, 0, 0)),
            ],
            out_specs=pl.BlockSpec((BLK, 8 * D), lambda g, b, *_: (b, g)),
            scratch_shapes=[
                pltpu.VMEM((13, 8 * BLK, 2 * BLK), jnp.float32),
                pltpu.VMEM((8 * BLK, BLK), jnp.float32),
                pltpu.VMEM((8 * BLK, BLK), jnp.float32),
                pltpu.VMEM((8 * BLK, D), jnp.float32),
            ],
        ),
        compiler_params=pltpu.CompilerParams(vmem_limit_bytes=VMEM_LIMIT),
        name="attend",
    )(segs, place, q2, kv)


def swap_kernel(mine, out, lsem, ssem, rsem):
    dp, ctx = lax.axis_index("dp"), lax.axis_index("ctx")
    core = ctx % 2
    sib = (dp, ctx + 1 - 2 * core)
    barrier = pltpu.get_barrier_semaphore()
    pl.semaphore_signal(barrier, inc=1, device_id=sib, device_id_type=MESH)
    pl.semaphore_wait(barrier, 1)
    cols = pl.ds(pl.multiple_of(core * 2048, 2048), 2048)
    others = pl.ds(pl.multiple_of((1 - core) * 2048, 2048), 2048)
    local = pltpu.make_async_copy(mine.at[pl.ds(pl.multiple_of(core * 256, 256), 256)], out.at[:, cols], lsem)
    src = mine.at[pl.ds(pl.multiple_of((1 - core) * 256, 256), 256)]
    remote = pltpu.make_async_remote_copy(src, out.at[:, cols], ssem, rsem, device_id=sib, device_id_type=MESH)
    landed = pltpu.make_async_remote_copy(src, out.at[:, others], ssem, rsem, device_id=sib, device_id_type=MESH)
    remote.start()
    local.start()
    local.wait()
    remote.wait_send()
    landed.wait_recv()


def swapped(mine):
    anywhere = pl.BlockSpec(memory_space=pl.ANY)
    return pl.pallas_call(
        swap_kernel,
        out_shape=jax.ShapeDtypeStruct((256, 4096), jnp.bfloat16),
        in_specs=[anywhere],
        out_specs=anywhere,
        scratch_shapes=[pltpu.SemaphoreType.DMA, pltpu.SemaphoreType.DMA, pltpu.SemaphoreType.DMA],
        compiler_params=pltpu.CompilerParams(collective_id=1, has_side_effects=True),
        name="swap",
    )(mine)


def body(hidden_in, queries, wk, wv, bk, bv, segs):
    ctx = lax.axis_index("ctx")
    cos, sin = rope_tables((ctx // 2) * 512, 512)
    kv, q2 = gathered(hidden_in[0], queries[0], wk, wv, bk.reshape(4, 1, D), bv.reshape(4, 1, D), cos, sin)
    place = jnp.reshape((ctx // 2) * 4, (1,)).astype(jnp.int32)
    mine = attended(segs[0], place, q2, kv.reshape(2, 4096, 256))
    return swapped(mine)[None]


def solution(mesh):
    placed = (P("dp", "ctx", None), P("dp", "ctx", None), P("dp", None), P("dp", None), P(), P(), P("dp", None))
    return jax.shard_map(body, mesh=mesh, in_specs=placed, out_specs=P("dp", "ctx", None), check_vma=False)
```

```python
import functools
import math

import jax
import jax.numpy as jnp
from jax import lax
from jax.experimental import pallas as pl
from jax.experimental.pallas import tpu as pltpu
from jax.sharding import PartitionSpec as P

MESH = pl.DeviceIdType.MESH
D = 128
BLK = 128
NBLK = 32
MOST = 12
ROPE_BASE = 1000000.0
BIG = 1e30
SCALE = math.log2(math.e) / math.sqrt(D)
VMEM_LIMIT = 56 * 1024 * 1024


def rope_tables(first, count):
    half = D // 2
    frequency = ROPE_BASE ** (-(jnp.arange(half, dtype=jnp.float32) * 2.0 / D))
    positions = (first + jnp.arange(count, dtype=jnp.int32)).astype(jnp.float32)
    angles = positions[:, None] * frequency[None, :]
    cos, sin = jnp.cos(angles), jnp.sin(angles)
    return jnp.concatenate([cos, cos], axis=1), jnp.concatenate([-sin, sin], axis=1)


def whole_kernel(
    slots, biases, hid, q, wk, wv, bk, bv, cos, sin, out,
    hbuf, wbuf, acc, kv0, kv1, q2, scores, peak, total, weighted, tiles,
    lsem, hsend, hrecv, wsend, wrecv, ksend, krecv, osend, orecv,
):
    kv = (kv0, kv1)
    dp, ctx = lax.axis_index("dp"), lax.axis_index("ctx")
    x, zh = dp // 4, dp % 4
    zl, y, core = ctx // 8, (ctx // 2) % 4, ctx % 2
    z = 2 * zh + zl
    m = zl * 4 + y

    def zdev(at):
        return (x * 4 + at // 2, (at % 2) * 8 + ctx % 8)

    xp, xm = (((x + 1) % 4) * 4 + zh, ctx), (((x + 3) % 4) * 4 + zh, ctx)
    zp, zm = zdev((z + 1) % 8), zdev((z + 7) % 8)
    yp = (dp, zl * 8 + ((y + 1) % 4) * 2 + core)
    ym = (dp, zl * 8 + ((y + 3) % 4) * 2 + core)
    sib = (dp, ctx + 1 - 2 * core)
    neighbours = (xp, xm, zp, zm, yp, ym, sib)

    def weights_in(g, which):
        head = pl.multiple_of((2 * core + g) * D, D)
        src = (wk, wv)[which].at[:, pl.ds(head, D)]
        return pltpu.make_async_copy(src, wbuf.at[g, dp, :, pl.ds(which * D, D)], lsem.at[2 * g + which])

    def hidden_in(j):
        at = (x + j) % 4
        cols = pl.ds(pl.multiple_of(at * 2048, 2048), 2048)
        rows = pl.ds(pl.multiple_of(core * 256, 256), 256)
        local = pltpu.make_async_copy(hid.at[:, cols], hbuf.at[at, rows], lsem.at[4 + j])
        remote = pltpu.make_async_remote_copy(
            hid.at[:, cols], hbuf.at[at, rows], hsend.at[j], hrecv.at[j], device_id=sib, device_id_type=MESH)
        return local, remote

    def hidden_landed(j):
        at = (x + j) % 4
        cols = pl.ds(pl.multiple_of(at * 2048, 2048), 2048)
        rows = pl.ds(pl.multiple_of((1 - core) * 256, 256), 256)
        return pltpu.make_async_remote_copy(
            hid.at[:, cols], hbuf.at[at, rows], hsend.at[j], hrecv.at[j], device_id=sib, device_id_type=MESH)

    my_rows = pl.ds(pl.multiple_of(core * 256, 256), 256)
    q_local = pltpu.make_async_copy(
        q.at[:, pl.ds(pl.multiple_of(core * 2048, 2048), 2048)], q2.at[my_rows], lsem.at[8])
    q_remote = pltpu.make_async_remote_copy(
        q.at[:, pl.ds(pl.multiple_of((1 - core) * 2048, 2048), 2048)], q2.at[my_rows],
        hsend.at[4], hrecv.at[4], device_id=sib, device_id_type=MESH)

    for g in range(2):
        for which in range(2):
            weights_in(g, which).start()

    barrier = pltpu.get_barrier_semaphore()
    for to in neighbours:
        pl.semaphore_signal(barrier, inc=1, device_id=to, device_id_type=MESH)
    pl.semaphore_wait(barrier, len(neighbours))

    turn = 1 - 2 * zl
    near_z, far_z, across_z = (zh + 4 - turn) % 4, (zh + turn + 4) % 4, (zh + 2) % 4
    before_x, after_x, across_x = (x + 3) % 4, (x + 1) % 4, (x + 2) % 4
    z_places, x_places = (zh, near_z, far_z, across_z), (x, before_x, after_x, across_x)
    near_dev = zdev((z + 8 - turn) % 8)
    far_dev = zdev((z + 8 + turn) % 8)

    def copy(g, shard, start, size, to, task, kind):
        ref = wbuf.at[g, shard, pl.ds(start, size)]
        at = (g * 10 + task) * 4 + kind
        return pltpu.make_async_remote_copy(
            ref, ref, wsend.at[at], wrecv.at[at], device_id=to, device_id_type=MESH)

    def x_base(k):
        return (z_places[max(k - 1, 0)], 0 if k == 0 else 256)

    def z_base(k):
        return (x_places[max(k - 1, 0)], 256 if k == 0 else 0)

    def x_start(g, k):
        at, base = x_base(k)
        for kind, to in ((0, xp), (1, xm)):
            copy(g, x * 4 + at, base, 256, to, k, kind).start()

    def x_level(g, k, level):
        at, base = x_base(k)
        if level == 1:
            for kind, place, to in ((0, before_x, xp), (1, after_x, xm)):
                shard = place * 4 + at
                copy(g, shard, base, 256, to, k, kind).wait_recv()
                copy(g, shard, base + 128 * kind, 128, to, k, kind + 2).start()
        else:
            shard = across_x * 4 + at
            for kind in range(2):
                copy(g, shard, base + 128 * kind, 128, xp, k, kind + 2).wait_recv()

    def z_start(g, k):
        at, base = z_base(k)
        copy(g, at * 4 + zh, base, 256, near_dev, k + 5, 0).start()

    def z_level(g, k, level):
        at, base = z_base(k)
        mine, theirs = base + 128 * zl, base + 128 * (1 - zl)
        if level == 1:
            copy(g, at * 4 + near_z, base, 256, near_dev, k + 5, 0).wait_recv()
            copy(g, at * 4 + near_z, base, 256, far_dev, k + 5, 1).start()
        elif level == 2:
            copy(g, at * 4 + far_z, base, 256, near_dev, k + 5, 1).wait_recv()
            start = pl.multiple_of(theirs, 128)
            copy(g, at * 4 + far_z, start, 128, near_dev, k + 5, 2).start()
        elif level == 3:
            start = pl.multiple_of(mine, 128)
            copy(g, at * 4 + across_z, start, 128, near_dev, k + 5, 2).wait_recv()
            copy(g, at * 4 + across_z, start, 128, far_dev, k + 5, 3).start()
        else:
            start = pl.multiple_of(theirs, 128)
            copy(g, at * 4 + across_z, start, 128, near_dev, k + 5, 3).wait_recv()

    def begin(g):
        weights_in(g, 0).wait()
        weights_in(g, 1).wait()
        for k in range(2):
            z_start(g, k)
            x_start(g, k)

    def step(g, r):
        events = (
            (("x", 0, 1, "z2", "z3"), ("z", 0, 1, "x2"), ("x", 1, 1), ("z", 1, 1)),
            (("x", 0, 2, "z4"), ("z", 0, 2, "x3"), ("z", 1, 2), ("x", 1, 2), ("z", 2, 1), ("z", 3, 1), ("x", 2, 1)),
            (("z", 0, 3), ("z", 1, 3), ("z", 2, 2), ("z", 3, 2), ("z", 4, 1), ("x", 3, 1), ("x", 2, 2)),
            (("z", 0, 4, "x4"), ("z", 1, 4), ("z", 2, 3), ("z", 3, 3), ("z", 4, 2), ("x", 3, 2)),
            (("x", 4, 1), ("z", 4, 3), ("z", 2, 4), ("z", 3, 4)),
            (("x", 4, 2), ("z", 4, 4)),
        )[r - 1]
        for axis, k, level, *then in events:
            (x_level if axis == "x" else z_level)(g, k, level)
            for name in then:
                (x_start if name[0] == "x" else z_start)(g, int(name[1]))

    def product(g, sx, sz, base):
        return jnp.dot(
            hbuf[sx, :, pl.ds(pl.multiple_of(sz * 512 + base, 256), 256)],
            wbuf[g, sx * 4 + sz, pl.ds(base, 256)],
            preferred_element_type=jnp.float32,
        )

    def multiply(g, tasks):
        sums = acc[...]
        for name in tasks:
            k = int(name[1])
            if name[0] == "x":
                at, base = x_base(k)
                for place in x_places[1:]:
                    sums += product(g, place, at, base)
            else:
                at, base = z_base(k)
                for place in z_places[1:]:
                    sums += product(g, at, place, base)
        acc[...] = sums

    def own(g):
        acc[...] = product(g, x, zh, 0) + product(g, x, zh, 256)

    def kcopy(g, at, kind, unit, to):
        start, size = (2 if kind == 3 else 0), (4 if kind < 2 else 2)
        ref = kv[g].at[pl.ds(unit * 4 + start, size)]
        n = g * 9 + at + kind
        return pltpu.make_async_remote_copy(ref, ref, ksend.at[n], krecv.at[n], device_id=to, device_id_type=MESH)

    def k_send(g, line, kind):
        unit = line * 4 + (y + (0, 0, 3, 1)[kind]) % 4
        at = 4 if isinstance(line, int) else 0
        kcopy(g, at, kind, unit, (yp, ym)[kind % 2]).start()

    def k_wait(g, line, kind):
        unit = line * 4 + (y + (3, 1, 2, 2)[kind]) % 4
        at = 4 if isinstance(line, int) else 0
        kcopy(g, at, kind, unit, yp).wait_recv()

    def cross(g, unit):
        ref = kv[g].at[pl.ds(unit * 4, 4)]
        n = g * 9 + 8
        to = (dp, ctx % 8 + 8)
        return pltpu.make_async_remote_copy(ref, ref, ksend.at[n], krecv.at[n], device_id=to, device_id_type=MESH)

    def kv_begin(g):
        sums = acc[...]
        head = 2 * core + g
        key = sums[:, :D] + bk[head]
        turned = jnp.concatenate([key[:, D // 2:], key[:, : D // 2]], axis=1)
        key = key * cos[...] + turned * sin[...]
        value = sums[:, D:] + bv[head]
        kv[g][pl.ds(m * 4, 4)] = jnp.concatenate([key, value], axis=1).astype(jnp.bfloat16).reshape(4, BLK, 2 * D)

        @pl.when(zl == 0)
        def _():
            cross(g, m).start()
        k_send(g, zl, 0)
        k_send(g, zl, 1)

    def kv_one(g):
        for kind in range(2):
            k_wait(g, zl, kind)
            k_send(g, zl, kind + 2)

        @pl.when(zl == 1)
        def _():
            cross(g, y).wait_recv()
            k_send(g, 0, 0)
            k_send(g, 0, 1)

    def kv_two(g):
        k_wait(g, zl, 2)
        k_wait(g, zl, 3)

        @pl.when(zl == 1)
        def _():
            for kind in range(2):
                k_wait(g, 0, kind)
                k_send(g, 0, kind + 2)

    def kv_three(g):
        @pl.when(zl == 1)
        def _():
            k_wait(g, 0, 2)
            k_wait(g, 0, 3)

    def kv_sent(g):
        for kind in range(4):
            kcopy(g, 0, kind, m, yp).wait_send()

        @pl.when(zl == 1)
        def _():
            for kind in range(4):
                kcopy(g, 4, kind, m, yp).wait_send()

        @pl.when(zl == 0)
        def _():
            cross(g, m).wait_send()

    begin(0)
    for j in (0, 1, 3, 2):
        local, remote = hidden_in(j)
        local.start()
        remote.start()
    q_local.start()
    q_remote.start()
    step(0, 1)
    step(0, 2)
    step(0, 3)
    begin(1)
    step(0, 4)
    for j in (0, 1, 3, 2):
        hidden_in(j)[0].wait()
        hidden_landed(j).wait_recv()
    own(0)
    multiply(0, ("x0", "x1", "z0", "z1"))
    step(1, 1)
    step(0, 5)
    multiply(0, ("x2", "x3", "z2", "z3"))
    step(1, 2)
    step(0, 6)
    multiply(0, ("x4", "z4"))
    kv_begin(0)
    step(1, 3)
    own(1)
    multiply(1, ("x0", "x1"))
    kv_one(0)
    step(1, 4)
    multiply(1, ("z0", "z1"))
    kv_two(0)
    step(1, 5)
    multiply(1, ("x2", "x3", "z2", "z3"))
    kv_three(0)
    step(1, 6)
    multiply(1, ("x4", "z4"))
    kv_begin(1)

    q_local.wait()
    others = pl.ds(pl.multiple_of((1 - core) * 256, 256), 256)
    pltpu.make_async_remote_copy(
        q.at[:, pl.ds(0, 2048)], q2.at[others], hsend.at[4], hrecv.at[4], device_id=sib, device_id_type=MESH).wait_recv()

    def attend(g, i):
        b = (i + 2 * (1 - core)) % 4
        t = m * 4 + b
        most = jnp.minimum(t, 2 * MOST - 1) // 2
        q_rows = pl.ds(pl.multiple_of(b * BLK, BLK), BLK)

        peak[...] = jnp.full_like(peak, -BIG)

        def score(c, first, second, less, mask):
            keys = jnp.concatenate([kv[g][first, :, :D], kv[g][second, :, :D]], axis=0)
            for j in range(8):
                rows = pl.ds(j * BLK, BLK)
                s = lax.dot_general(
                    q2[q_rows, g * 1024 + j * D:g * 1024 + (j + 1) * D], keys, (((1,), (1,)), ((), ())),
                    preferred_element_type=jnp.float32) * SCALE
                if mask is not None:
                    s = jnp.where(mask, s, -BIG)
                scores[c, rows] = s
                top = jnp.maximum(s[:, :BLK], s[:, BLK:])
                if mask is None:
                    top = top - less
                peak[rows] = jnp.maximum(peak[rows], top)

        def one(c, carry):
            score(c, slots[b, 2 * c], slots[b, 2 * c + 1], biases[b, c], None)
            return carry

        lax.fori_loop(0, most, one, 0)
        extra, from_row = slots[b, 24], slots[b, 25]
        row = lax.broadcasted_iota(jnp.int32, (BLK, 2 * BLK), 0)
        col = lax.broadcasted_iota(jnp.int32, (BLK, 2 * BLK), 1)
        least = jnp.where(col < BLK, from_row, col - BLK)
        score(most, extra, t, 0.0, row >= least)

        peak[...] = jnp.broadcast_to(jnp.max(peak[...], axis=1, keepdims=True), peak.shape)
        total[...] = jnp.zeros_like(total)
        weighted[...] = jnp.zeros_like(weighted)

        def weigh(c, first, second, less):
            values = jnp.concatenate([kv[g][first, :, D:], kv[g][second, :, D:]], axis=0)
            for j in range(8):
                rows = pl.ds(j * BLK, BLK)
                top = peak[rows] + less
                left = jnp.exp2(scores[c, rows, :BLK] - top)
                right = jnp.exp2(scores[c, rows, BLK:] - top)
                total[rows] += left + right
                weights = jnp.concatenate([left, right], axis=1).astype(jnp.bfloat16)
                weighted[rows] += jnp.dot(weights, values, preferred_element_type=jnp.float32)

        def two(c, carry):
            weigh(c, slots[b, 2 * c], slots[b, 2 * c + 1], biases[b, c])
            return carry

        lax.fori_loop(0, most, two, 0)
        weigh(most, extra, t, 0.0)
        for j in range(8):
            rows = pl.ds(j * BLK, BLK)
            tiles[g * 4 + i, :, j * D:(j + 1) * D] = (
                weighted[rows] / jnp.sum(total[rows], axis=1, keepdims=True)).astype(jnp.bfloat16)

    def leaving(g, i):
        cols = pl.ds(pl.multiple_of(core * 2048 + g * 1024, 1024), 1024)
        src, dst = tiles.at[g * 4 + i], out.at[(i % 2) * BLK:(i % 2 + 1) * BLK, cols]
        if i < 2:
            return pltpu.make_async_remote_copy(
                src, dst, osend.at[g * 2 + i], orecv.at[g * 2 + i], device_id=sib, device_id_type=MESH)
        return pltpu.make_async_copy(src, dst, lsem.at[9 + g * 2 + i - 2])

    def coming(g, i):
        cols = pl.ds(pl.multiple_of((1 - core) * 2048 + g * 1024, 1024), 1024)
        return pltpu.make_async_remote_copy(
            tiles.at[g * 4 + i], out.at[i * BLK:(i + 1) * BLK, cols], osend.at[g * 2 + i], orecv.at[g * 2 + i],
            device_id=sib, device_id_type=MESH)

    attend(0, 0)
    leaving(0, 0).start()
    kv_one(1)
    attend(0, 1)
    leaving(0, 1).start()
    kv_two(1)
    attend(0, 2)
    leaving(0, 2).start()
    kv_three(1)
    attend(0, 3)
    leaving(0, 3).start()
    for i in range(4):
        attend(1, i)
        leaving(1, i).start()

    def drain(at, carry):
        for kind in range(4):
            n = at * 4 + kind
            rows = pl.ds(0, 256 if kind < 2 else 128)
            ref = wbuf.at[0, 0, rows]
            pltpu.make_async_remote_copy(
                ref, ref, wsend.at[n], wrecv.at[n], device_id=xp, device_id_type=MESH).wait_send()
        return carry

    lax.fori_loop(0, 20, drain, 0)
    for g in range(2):
        kv_sent(g)
    for j in range(4):
        hidden_in(j)[1].wait_send()
    q_remote.wait_send()
    for g in range(2):
        for i in range(2):
            leaving(g, i).wait_send()
            coming(g, i).wait_recv()
            leaving(g, i + 2).wait()


def attended(slots, biases, hid, q, wk, wv, bk, bv, cos, sin):
    vmem, anywhere = pl.BlockSpec(memory_space=pltpu.VMEM), pl.BlockSpec(memory_space=pl.ANY)
    smem = pl.BlockSpec(memory_space=pltpu.SMEM)
    bf16, f32, dma = jnp.bfloat16, jnp.float32, pltpu.SemaphoreType.DMA
    return pl.pallas_call(
        whole_kernel,
        out_shape=jax.ShapeDtypeStruct((256, 4096), bf16),
        in_specs=[smem] * 2 + [anywhere] * 4 + [vmem] * 4,
        out_specs=anywhere,
        scratch_shapes=[
            pltpu.VMEM((4, 512, 2048), bf16),
            pltpu.VMEM((2, 16, 512, 256), bf16),
            pltpu.VMEM((512, 256), f32),
            pltpu.VMEM((NBLK, BLK, 2 * D), bf16),
            pltpu.VMEM((NBLK, BLK, 2 * D), bf16),
            pltpu.VMEM((512, 2048), bf16),
            pltpu.VMEM((MOST, 8 * BLK, 2 * BLK), f32),
            pltpu.VMEM((8 * BLK, BLK), f32),
            pltpu.VMEM((8 * BLK, BLK), f32),
            pltpu.VMEM((8 * BLK, D), f32),
            pltpu.VMEM((8, BLK, 8 * D), bf16),
            dma((13,)), dma((5,)), dma((5,)), dma((80,)), dma((80,)), dma((18,)), dma((18,)), dma((4,)), dma((4,)),
        ],
        compiler_params=pltpu.CompilerParams(collective_id=0, has_side_effects=True, vmem_limit_bytes=VMEM_LIMIT),
        name="attended",
    )(slots, biases, hid, q, wk, wv, bk, bv, cos, sin)


def block_table(segs, first):
    t = first + jnp.arange(4, dtype=jnp.int32)
    at = jnp.arange(NBLK, dtype=jnp.int32)
    before = at[None, :] < t[:, None]
    mine = jnp.sum(jnp.where(at[None, :] == t[:, None], segs[None, :], 0), axis=1)
    premise = jnp.sum(before & (segs == 0)[None, :], axis=1, dtype=jnp.int32)
    own = jnp.sum(before & (segs[None, :] == mine[:, None]) & (segs != 0)[None, :], axis=1, dtype=jnp.int32)
    seen = premise + own

    def block(j):
        return jnp.minimum(jnp.where(j < premise[:, None], j, j - seen[:, None] + t[:, None]), t[:, None])

    j = jnp.arange(2 * MOST, dtype=jnp.int32)[None, :]
    extra = block(jnp.maximum(seen - 1, 0)[:, None])
    from_row = jnp.where(seen % 2 == 1, -1, BLK)[:, None]
    pairs = jnp.arange(MOST, dtype=jnp.int32)[None, :]
    biases = jnp.where(2 * pairs + 1 < seen[:, None], 0.0, BIG).astype(jnp.float32)
    return jnp.concatenate([block(j), extra, from_row], axis=1).astype(jnp.int32), biases


def body(hidden_in, queries, wk, wv, bk, bv, segs):
    chip = lax.axis_index("ctx") // 2
    cos, sin = rope_tables(chip * 512, 512)
    slots, biases = block_table(segs[0], chip * 4)
    return attended(
        slots, biases, hidden_in[0], queries[0], wk, wv, bk.reshape(4, 1, D), bv.reshape(4, 1, D), cos, sin)[None]


def solution(mesh):
    placed = (P("dp", "ctx", None), P("dp", "ctx", None), P("dp", None), P("dp", None), P(), P(), P("dp", None))
    return jax.shard_map(body, mesh=mesh, in_specs=placed, out_specs=P("dp", "ctx", None), check_vma=False)
```

```python
import math

import jax
import jax.numpy as jnp
from jax import lax
from jax.experimental import pallas as pl
from jax.experimental.pallas import tpu as pltpu
from jax.sharding import PartitionSpec as P

MESH = pl.DeviceIdType.MESH
D = 128
BLK = 128
NBLK = 32
MOST = 12
ROPE_BASE = 1000000.0
BIG = 1e30
SCALE = math.log2(math.e) / math.sqrt(D)
VMEM_LIMIT = 56 * 1024 * 1024


def rope_tables(first, count):
    half = D // 2
    frequency = ROPE_BASE ** (-(jnp.arange(half, dtype=jnp.float32) * 2.0 / D))
    positions = (first + jnp.arange(count, dtype=jnp.int32)).astype(jnp.float32)
    angles = positions[:, None] * frequency[None, :]
    cos, sin = jnp.cos(angles), jnp.sin(angles)
    return jnp.concatenate([cos, cos], axis=1), jnp.concatenate([-sin, sin], axis=1)


def whole_kernel(
    slots, biases, hid, q, wk, wv, bk, bv, cos, sin, out,
    hbuf, wbuf, acc, kv0, kv1, q2, scores0, scores1, peak0, peak1, total, weighted, tiles,
    lsem, hsend, hrecv, wsend, wrecv, ksend, krecv, osend, orecv,
):
    kv, scores, peaks = (kv0, kv1), (scores0, scores1), (peak0, peak1)
    dp, ctx = lax.axis_index("dp"), lax.axis_index("ctx")
    x, zh = dp // 4, dp % 4
    zl, y, core = ctx // 8, (ctx // 2) % 4, ctx % 2
    z = 2 * zh + zl
    m = zl * 4 + y

    def zdev(at):
        return (x * 4 + at // 2, (at % 2) * 8 + ctx % 8)

    xp, xm = (((x + 1) % 4) * 4 + zh, ctx), (((x + 3) % 4) * 4 + zh, ctx)
    zp, zm = zdev((z + 1) % 8), zdev((z + 7) % 8)
    yp = (dp, zl * 8 + ((y + 1) % 4) * 2 + core)
    ym = (dp, zl * 8 + ((y + 3) % 4) * 2 + core)
    sib = (dp, ctx + 1 - 2 * core)
    neighbours = (xp, xm, zp, zm, yp, ym, sib)

    def weights_in(g, which):
        head = pl.multiple_of((2 * core + g) * D, D)
        src = (wk, wv)[which].at[:, pl.ds(head, D)]
        return pltpu.make_async_copy(src, wbuf.at[g, dp, :, pl.ds(which * D, D)], lsem.at[2 * g + which])

    def hidden_in(j):
        at = (x + j) % 4
        cols = pl.ds(pl.multiple_of(at * 2048, 2048), 2048)
        rows = pl.ds(pl.multiple_of(core * 256, 256), 256)
        local = pltpu.make_async_copy(hid.at[:, cols], hbuf.at[at, rows], lsem.at[4 + j])
        remote = pltpu.make_async_remote_copy(
            hid.at[:, cols], hbuf.at[at, rows], hsend.at[j], hrecv.at[j], device_id=sib, device_id_type=MESH)
        return local, remote

    def hidden_landed(j):
        at = (x + j) % 4
        cols = pl.ds(pl.multiple_of(at * 2048, 2048), 2048)
        rows = pl.ds(pl.multiple_of((1 - core) * 256, 256), 256)
        return pltpu.make_async_remote_copy(
            hid.at[:, cols], hbuf.at[at, rows], hsend.at[j], hrecv.at[j], device_id=sib, device_id_type=MESH)

    my_rows = pl.ds(pl.multiple_of(core * 256, 256), 256)
    q_local = pltpu.make_async_copy(
        q.at[:, pl.ds(pl.multiple_of(core * 2048, 2048), 2048)], q2.at[my_rows], lsem.at[8])
    q_remote = pltpu.make_async_remote_copy(
        q.at[:, pl.ds(pl.multiple_of((1 - core) * 2048, 2048), 2048)], q2.at[my_rows],
        hsend.at[4], hrecv.at[4], device_id=sib, device_id_type=MESH)

    for g in range(2):
        for which in range(2):
            weights_in(g, which).start()

    barrier = pltpu.get_barrier_semaphore()
    for to in neighbours:
        pl.semaphore_signal(barrier, inc=1, device_id=to, device_id_type=MESH)
    pl.semaphore_wait(barrier, len(neighbours))

    turn = 1 - 2 * zl
    near_z, far_z, across_z = (zh + 4 - turn) % 4, (zh + turn + 4) % 4, (zh + 2) % 4
    before_x, after_x, across_x = (x + 3) % 4, (x + 1) % 4, (x + 2) % 4
    z_places, x_places = (zh, near_z, far_z, across_z), (x, before_x, after_x, across_x)
    near_dev = zdev((z + 8 - turn) % 8)
    far_dev = zdev((z + 8 + turn) % 8)

    def copy(g, shard, start, size, to, task, kind):
        ref = wbuf.at[g, shard, pl.ds(start, size)]
        at = (g * 10 + task) * 4 + kind
        return pltpu.make_async_remote_copy(
            ref, ref, wsend.at[at], wrecv.at[at], device_id=to, device_id_type=MESH)

    def x_base(k):
        return (z_places[max(k - 1, 0)], 0 if k == 0 else 256)

    def z_base(k):
        return (x_places[max(k - 1, 0)], 256 if k == 0 else 0)

    def x_start(g, k):
        at, base = x_base(k)
        for kind, to in ((0, xp), (1, xm)):
            copy(g, x * 4 + at, base, 256, to, k, kind).start()

    def x_level(g, k, level):
        at, base = x_base(k)
        if level == 1:
            for kind, place, to in ((0, before_x, xp), (1, after_x, xm)):
                shard = place * 4 + at
                copy(g, shard, base, 256, to, k, kind).wait_recv()
                copy(g, shard, base + 128 * kind, 128, to, k, kind + 2).start()
        else:
            shard = across_x * 4 + at
            for kind in range(2):
                copy(g, shard, base + 128 * kind, 128, xp, k, kind + 2).wait_recv()

    def z_start(g, k):
        at, base = z_base(k)
        copy(g, at * 4 + zh, base, 256, near_dev, k + 5, 0).start()

    def z_level(g, k, level):
        at, base = z_base(k)
        mine, theirs = base + 128 * zl, base + 128 * (1 - zl)
        if level == 1:
            copy(g, at * 4 + near_z, base, 256, near_dev, k + 5, 0).wait_recv()
            copy(g, at * 4 + near_z, base, 256, far_dev, k + 5, 1).start()
        elif level == 2:
            copy(g, at * 4 + far_z, base, 256, near_dev, k + 5, 1).wait_recv()
            start = pl.multiple_of(theirs, 128)
            copy(g, at * 4 + far_z, start, 128, near_dev, k + 5, 2).start()
        elif level == 3:
            start = pl.multiple_of(mine, 128)
            copy(g, at * 4 + across_z, start, 128, near_dev, k + 5, 2).wait_recv()
            copy(g, at * 4 + across_z, start, 128, far_dev, k + 5, 3).start()
        else:
            start = pl.multiple_of(theirs, 128)
            copy(g, at * 4 + across_z, start, 128, near_dev, k + 5, 3).wait_recv()

    def begin(g):
        weights_in(g, 0).wait()
        weights_in(g, 1).wait()
        for k in range(2):
            z_start(g, k)
            x_start(g, k)

    def step(g, r):
        events = (
            (("x", 0, 1, "z2", "z3"), ("z", 0, 1, "x2"), ("x", 1, 1), ("z", 1, 1)),
            (("x", 0, 2, "z4"), ("z", 0, 2, "x3"), ("z", 1, 2), ("x", 1, 2), ("z", 2, 1), ("z", 3, 1), ("x", 2, 1)),
            (("z", 0, 3), ("z", 1, 3), ("z", 2, 2), ("z", 3, 2), ("z", 4, 1), ("x", 3, 1), ("x", 2, 2)),
            (("z", 0, 4, "x4"), ("z", 1, 4), ("z", 2, 3), ("z", 3, 3), ("z", 4, 2), ("x", 3, 2)),
            (("x", 4, 1), ("z", 4, 3), ("z", 2, 4), ("z", 3, 4)),
            (("x", 4, 2), ("z", 4, 4)),
        )[r - 1]
        for axis, k, level, *then in events:
            (x_level if axis == "x" else z_level)(g, k, level)
            for name in then:
                (x_start if name[0] == "x" else z_start)(g, int(name[1]))

    def product(g, sx, sz, base):
        return jnp.dot(
            hbuf[sx, :, pl.ds(pl.multiple_of(sz * 512 + base, 256), 256)],
            wbuf[g, sx * 4 + sz, pl.ds(base, 256)],
            preferred_element_type=jnp.float32,
        )

    def multiply(g, tasks):
        sums = acc[...]
        for name in tasks:
            k = int(name[1])
            if name[0] == "x":
                at, base = x_base(k)
                for place in x_places[1:]:
                    sums += product(g, place, at, base)
            else:
                at, base = z_base(k)
                for place in z_places[1:]:
                    sums += product(g, at, place, base)
        acc[...] = sums

    def own(g):
        acc[...] = product(g, x, zh, 0) + product(g, x, zh, 256)

    def kcopy(g, at, kind, unit, to):
        start, size = (2 if kind == 3 else 0), (4 if kind < 2 else 2)
        ref = kv[g].at[pl.ds(unit * 4 + start, size)]
        n = g * 9 + at + kind
        return pltpu.make_async_remote_copy(ref, ref, ksend.at[n], krecv.at[n], device_id=to, device_id_type=MESH)

    def k_send(g, line, kind):
        unit = line * 4 + (y + (0, 0, 3, 1)[kind]) % 4
        at = 4 if isinstance(line, int) else 0
        kcopy(g, at, kind, unit, (yp, ym)[kind % 2]).start()

    def k_wait(g, line, kind):
        unit = line * 4 + (y + (3, 1, 2, 2)[kind]) % 4
        at = 4 if isinstance(line, int) else 0
        kcopy(g, at, kind, unit, yp).wait_recv()

    def cross(g, unit):
        ref = kv[g].at[pl.ds(unit * 4, 4)]
        n = g * 9 + 8
        to = (dp, ctx % 8 + 8)
        return pltpu.make_async_remote_copy(ref, ref, ksend.at[n], krecv.at[n], device_id=to, device_id_type=MESH)

    def kv_begin(g):
        sums = acc[...]
        head = 2 * core + g
        key = sums[:, :D] + bk[head]
        turned = jnp.concatenate([key[:, D // 2:], key[:, : D // 2]], axis=1)
        key = key * cos[...] + turned * sin[...]
        value = sums[:, D:] + bv[head]
        kv[g][pl.ds(m * 4, 4)] = jnp.concatenate([key, value], axis=1).astype(jnp.bfloat16).reshape(4, BLK, 2 * D)

        @pl.when(zl == 0)
        def _():
            cross(g, m).start()
        k_send(g, zl, 0)
        k_send(g, zl, 1)

    def kv_one(g):
        for kind in range(2):
            k_wait(g, zl, kind)
            k_send(g, zl, kind + 2)

        @pl.when(zl == 1)
        def _():
            cross(g, y).wait_recv()
            k_send(g, 0, 0)
            k_send(g, 0, 1)

    def kv_two(g):
        k_wait(g, zl, 2)
        k_wait(g, zl, 3)

        @pl.when(zl == 1)
        def _():
            for kind in range(2):
                k_wait(g, 0, kind)
                k_send(g, 0, kind + 2)

    def kv_three(g):
        @pl.when(zl == 1)
        def _():
            k_wait(g, 0, 2)
            k_wait(g, 0, 3)

    def kv_sent(g):
        for kind in range(4):
            kcopy(g, 0, kind, m, yp).wait_send()

        @pl.when(zl == 1)
        def _():
            for kind in range(4):
                kcopy(g, 4, kind, m, yp).wait_send()

        @pl.when(zl == 0)
        def _():
            cross(g, m).wait_send()

    begin(0)
    for j in (0, 1, 3, 2):
        local, remote = hidden_in(j)
        local.start()
        remote.start()
    q_local.start()
    q_remote.start()
    step(0, 1)
    step(0, 2)
    step(0, 3)
    begin(1)
    step(0, 4)
    for j in (0, 1, 3, 2):
        hidden_in(j)[0].wait()
        hidden_landed(j).wait_recv()
    own(0)
    multiply(0, ("x0", "x1", "z0", "z1"))
    step(1, 1)
    step(0, 5)
    multiply(0, ("x2", "x3", "z2", "z3"))
    step(1, 2)
    step(0, 6)
    multiply(0, ("x4", "z4"))
    kv_begin(0)
    step(1, 3)
    own(1)
    multiply(1, ("x0", "x1"))
    kv_one(0)
    step(1, 4)
    multiply(1, ("z0", "z1"))
    kv_two(0)
    step(1, 5)
    multiply(1, ("x2", "x3", "z2", "z3"))
    kv_three(0)

    q_local.wait()
    others = pl.ds(pl.multiple_of((1 - core) * 256, 256), 256)
    pltpu.make_async_remote_copy(
        q.at[:, pl.ds(0, 2048)], q2.at[others], hsend.at[4], hrecv.at[4], device_id=sib, device_id_type=MESH).wait_recv()

    pairs = jnp.minimum(m * 4 + 3, 2 * MOST - 1) // 2
    row = lax.broadcasted_iota(jnp.int32, (BLK, 2 * BLK), 0)
    col = lax.broadcasted_iota(jnp.int32, (BLK, 2 * BLK), 1)

    def block_of(i):
        return (i + 2 * (1 - core)) % 4

    def stage(done, ahead):
        order = lambda tile: (tile[0] * 4 + tile[1]) % 2
        if done is not None:
            g_done, b_done, top_ref, s_done = done[0], block_of(done[1]), peaks[order(done)], scores[order(done)]
            top_ref[...] = jnp.broadcast_to(jnp.max(top_ref[...], axis=1, keepdims=True), top_ref.shape)
            total[...] = jnp.zeros_like(total)
            weighted[...] = jnp.zeros_like(weighted)
        if ahead is not None:
            g_ahead, b_ahead, peak_ref, s_ahead = ahead[0], block_of(ahead[1]), peaks[order(ahead)], scores[order(ahead)]
            peak_ref[...] = jnp.full_like(peak_ref, -BIG)
            q_rows = pl.ds(pl.multiple_of(b_ahead * BLK, BLK), BLK)

        def places(b, c, last):
            if last:
                return slots[b, 24], m * 4 + b, 0.0
            return slots[b, 2 * c], slots[b, 2 * c + 1], biases[b, c]

        def two(c0, ends):
            for j in range(8):
                rows = pl.ds(j * BLK, BLK)
                best, share, mixed = None, 0.0, 0.0
                for u in range(2):
                    c, last = c0 + u, ends and u == 1
                    if ahead is not None:
                        first, second, less = places(b_ahead, c, last)
                        keys = jnp.concatenate([kv[g_ahead][first, :, :D], kv[g_ahead][second, :, :D]], axis=0)
                        s = lax.dot_general(
                            q2[q_rows, g_ahead * 1024 + j * D:g_ahead * 1024 + (j + 1) * D], keys,
                            (((1,), (1,)), ((), ())), preferred_element_type=jnp.float32) * SCALE
                        if last:
                            least = jnp.where(col < BLK, slots[b_ahead, 25], col - BLK)
                            s = jnp.where(row >= least, s, -BIG)
                        s_ahead[c, rows] = s
                        here = jnp.maximum(s[:, :BLK], s[:, BLK:])
                        if not last:
                            here = here - less
                        best = here if best is None else jnp.maximum(best, here)
                    if done is not None:
                        first, second, less = places(b_done, c, last)
                        values = jnp.concatenate([kv[g_done][first, :, D:], kv[g_done][second, :, D:]], axis=0)
                        top = top_ref[rows] if last else top_ref[rows] + less
                        left = jnp.exp2(s_done[c, rows, :BLK] - top)
                        right = jnp.exp2(s_done[c, rows, BLK:] - top)
                        share += left + right
                        weights = jnp.concatenate([left, right], axis=1).astype(jnp.bfloat16)
                        mixed += jnp.dot(weights, values, preferred_element_type=jnp.float32)
                if ahead is not None:
                    peak_ref[rows] = jnp.maximum(peak_ref[rows], best)
                if done is not None:
                    total[rows] += share
                    weighted[rows] += mixed

        def main(c, carry):
            two(2 * c, False)
            return carry

        lax.fori_loop(0, (pairs - 1) // 2, main, 0)
        two(pairs - 1, True)
        if done is not None:
            at = done[0] * 4 + done[1]
            for j in range(8):
                rows = pl.ds(j * BLK, BLK)
                tiles[at, :, j * D:(j + 1) * D] = (
                    weighted[rows] / jnp.sum(total[rows], axis=1, keepdims=True)).astype(jnp.bfloat16)
            leaving(*done).start()

    def leaving(g, i):
        cols = pl.ds(pl.multiple_of(core * 2048 + g * 1024, 1024), 1024)
        src, dst = tiles.at[g * 4 + i], out.at[(i % 2) * BLK:(i % 2 + 1) * BLK, cols]
        if i < 2:
            return pltpu.make_async_remote_copy(
                src, dst, osend.at[g * 2 + i], orecv.at[g * 2 + i], device_id=sib, device_id_type=MESH)
        return pltpu.make_async_copy(src, dst, lsem.at[9 + g * 2 + i - 2])

    def coming(g, i):
        cols = pl.ds(pl.multiple_of((1 - core) * 2048 + g * 1024, 1024), 1024)
        return pltpu.make_async_remote_copy(
            tiles.at[g * 4 + i], out.at[i * BLK:(i + 1) * BLK, cols], osend.at[g * 2 + i], orecv.at[g * 2 + i],
            device_id=sib, device_id_type=MESH)

    step(1, 6)
    multiply(1, ("x4", "z4"))
    kv_begin(1)
    stage(None, (0, 0))
    stage((0, 0), (0, 1))
    kv_one(1)
    stage((0, 1), (0, 2))
    kv_two(1)
    stage((0, 2), (0, 3))
    kv_three(1)
    stage((0, 3), (1, 0))
    for i in range(3):
        stage((1, i), (1, i + 1))
    stage((1, 3), None)

    def drain(at, carry):
        for kind in range(4):
            n = at * 4 + kind
            rows = pl.ds(0, 256 if kind < 2 else 128)
            ref = wbuf.at[0, 0, rows]
            pltpu.make_async_remote_copy(
                ref, ref, wsend.at[n], wrecv.at[n], device_id=xp, device_id_type=MESH).wait_send()
        return carry

    lax.fori_loop(0, 20, drain, 0)
    for g in range(2):
        kv_sent(g)
    for j in range(4):
        hidden_in(j)[1].wait_send()
    q_remote.wait_send()
    for g in range(2):
        for i in range(2):
            leaving(g, i).wait_send()
            coming(g, i).wait_recv()
            leaving(g, i + 2).wait()


def attended(slots, biases, hid, q, wk, wv, bk, bv, cos, sin):
    vmem, anywhere = pl.BlockSpec(memory_space=pltpu.VMEM), pl.BlockSpec(memory_space=pl.ANY)
    smem = pl.BlockSpec(memory_space=pltpu.SMEM)
    bf16, f32, dma = jnp.bfloat16, jnp.float32, pltpu.SemaphoreType.DMA
    return pl.pallas_call(
        whole_kernel,
        out_shape=jax.ShapeDtypeStruct((256, 4096), bf16),
        in_specs=[smem] * 2 + [anywhere] * 4 + [vmem] * 4,
        out_specs=anywhere,
        scratch_shapes=[
            pltpu.VMEM((4, 512, 2048), bf16),
            pltpu.VMEM((2, 16, 512, 256), bf16),
            pltpu.VMEM((512, 256), f32),
            pltpu.VMEM((NBLK, BLK, 2 * D), bf16),
            pltpu.VMEM((NBLK, BLK, 2 * D), bf16),
            pltpu.VMEM((512, 2048), bf16),
            pltpu.VMEM((MOST, 8 * BLK, 2 * BLK), f32),
            pltpu.VMEM((MOST, 8 * BLK, 2 * BLK), f32),
            pltpu.VMEM((8 * BLK, BLK), f32),
            pltpu.VMEM((8 * BLK, BLK), f32),
            pltpu.VMEM((8 * BLK, BLK), f32),
            pltpu.VMEM((8 * BLK, D), f32),
            pltpu.VMEM((8, BLK, 8 * D), bf16),
            dma((13,)), dma((5,)), dma((5,)), dma((80,)), dma((80,)), dma((18,)), dma((18,)), dma((4,)), dma((4,)),
        ],
        compiler_params=pltpu.CompilerParams(collective_id=0, has_side_effects=True, vmem_limit_bytes=VMEM_LIMIT),
        name="attended",
    )(slots, biases, hid, q, wk, wv, bk, bv, cos, sin)


def block_table(segs, first):
    t = first + jnp.arange(4, dtype=jnp.int32)
    at = jnp.arange(NBLK, dtype=jnp.int32)
    before = at[None, :] < t[:, None]
    mine = jnp.sum(jnp.where(at[None, :] == t[:, None], segs[None, :], 0), axis=1)
    premise = jnp.sum(before & (segs == 0)[None, :], axis=1, dtype=jnp.int32)
    own = jnp.sum(before & (segs[None, :] == mine[:, None]) & (segs != 0)[None, :], axis=1, dtype=jnp.int32)
    seen = premise + own

    def block(j):
        return jnp.minimum(jnp.where(j < premise[:, None], j, j - seen[:, None] + t[:, None]), t[:, None])

    j = jnp.arange(2 * MOST, dtype=jnp.int32)[None, :]
    extra = block(jnp.maximum(seen - 1, 0)[:, None])
    from_row = jnp.where(seen % 2 == 1, -1, BLK)[:, None]
    pairs = jnp.arange(MOST, dtype=jnp.int32)[None, :]
    biases = jnp.where(2 * pairs + 1 < seen[:, None], 0.0, BIG).astype(jnp.float32)
    return jnp.concatenate([block(j), extra, from_row], axis=1).astype(jnp.int32), biases


def body(hidden_in, queries, wk, wv, bk, bv, segs):
    chip = lax.axis_index("ctx") // 2
    cos, sin = rope_tables(chip * 512, 512)
    slots, biases = block_table(segs[0], chip * 4)
    return attended(
        slots, biases, hidden_in[0], queries[0], wk, wv, bk.reshape(4, 1, D), bv.reshape(4, 1, D), cos, sin)[None]


def solution(mesh):
    placed = (P("dp", "ctx", None), P("dp", "ctx", None), P("dp", None), P("dp", None), P(), P(), P("dp", None))
    return jax.shard_map(body, mesh=mesh, in_specs=placed, out_specs=P("dp", "ctx", None), check_vma=False)
```

```python
import math

import jax
import jax.numpy as jnp
from jax import lax
from jax.experimental import pallas as pl
from jax.experimental.pallas import tpu as pltpu
from jax.sharding import PartitionSpec as P

MESH = pl.DeviceIdType.MESH
D = 128
BLK = 128
NBLK = 32
MOST = 12
ROPE_BASE = 1000000.0
BIG = 1e30
SCALE = math.log2(math.e) / math.sqrt(D)
VMEM_LIMIT = 56 * 1024 * 1024


def whole_kernel(
    slots, biases, hid, q, wk, wv, bk, bv, frequency, out,
    cos, sin, hbuf, wbuf, acc, kv0, kv1, q2, scores0, scores1, peak0, peak1, total, weighted, tiles,
    lsem, hsend, hrecv, wsend, wrecv, ksend, krecv, osend, orecv,
):
    kv, scores, peaks = (kv0, kv1), (scores0, scores1), (peak0, peak1)
    dp, ctx = lax.axis_index("dp"), lax.axis_index("ctx")
    x, zh = dp // 4, dp % 4
    zl, y, core = ctx // 8, (ctx // 2) % 4, ctx % 2
    z = 2 * zh + zl
    m = zl * 4 + y

    def zdev(at):
        return (x * 4 + at // 2, (at % 2) * 8 + ctx % 8)

    xp, xm = (((x + 1) % 4) * 4 + zh, ctx), (((x + 3) % 4) * 4 + zh, ctx)
    zp, zm = zdev((z + 1) % 8), zdev((z + 7) % 8)
    yp = (dp, zl * 8 + ((y + 1) % 4) * 2 + core)
    ym = (dp, zl * 8 + ((y + 3) % 4) * 2 + core)
    sib = (dp, ctx + 1 - 2 * core)
    neighbours = (xp, xm, zp, zm, yp, ym, sib)

    def weights_in(g, which):
        head = pl.multiple_of((2 * core + g) * D, D)
        src = (wk, wv)[which].at[:, pl.ds(head, D)]
        return pltpu.make_async_copy(src, wbuf.at[g, dp, :, pl.ds(which * D, D)], lsem.at[2 * g + which])

    def hidden_in(j):
        at = (x + j) % 4
        cols = pl.ds(pl.multiple_of(at * 2048, 2048), 2048)
        rows = pl.ds(pl.multiple_of(core * 256, 256), 256)
        local = pltpu.make_async_copy(hid.at[:, cols], hbuf.at[at, rows], lsem.at[4 + j])
        remote = pltpu.make_async_remote_copy(
            hid.at[:, cols], hbuf.at[at, rows], hsend.at[j], hrecv.at[j], device_id=sib, device_id_type=MESH)
        return local, remote

    def hidden_landed(j):
        at = (x + j) % 4
        cols = pl.ds(pl.multiple_of(at * 2048, 2048), 2048)
        rows = pl.ds(pl.multiple_of((1 - core) * 256, 256), 256)
        return pltpu.make_async_remote_copy(
            hid.at[:, cols], hbuf.at[at, rows], hsend.at[j], hrecv.at[j], device_id=sib, device_id_type=MESH)

    my_rows = pl.ds(pl.multiple_of(core * 256, 256), 256)
    q_local = pltpu.make_async_copy(
        q.at[:, pl.ds(pl.multiple_of(core * 2048, 2048), 2048)], q2.at[my_rows], lsem.at[8])
    q_remote = pltpu.make_async_remote_copy(
        q.at[:, pl.ds(pl.multiple_of((1 - core) * 2048, 2048), 2048)], q2.at[my_rows],
        hsend.at[4], hrecv.at[4], device_id=sib, device_id_type=MESH)

    for g in range(2):
        for which in range(2):
            weights_in(g, which).start()

    barrier = pltpu.get_barrier_semaphore()
    for to in neighbours:
        pl.semaphore_signal(barrier, inc=1, device_id=to, device_id_type=MESH)
    pl.semaphore_wait(barrier, len(neighbours))

    turn = 1 - 2 * zl
    near_z, far_z, across_z = (zh + 4 - turn) % 4, (zh + turn + 4) % 4, (zh + 2) % 4
    before_x, after_x, across_x = (x + 3) % 4, (x + 1) % 4, (x + 2) % 4
    z_places, x_places = (zh, near_z, far_z, across_z), (x, before_x, after_x, across_x)
    near_dev = zdev((z + 8 - turn) % 8)
    far_dev = zdev((z + 8 + turn) % 8)

    def copy(g, shard, start, size, to, task, kind):
        ref = wbuf.at[g, shard, pl.ds(start, size)]
        at = (g * 10 + task) * 4 + kind
        return pltpu.make_async_remote_copy(
            ref, ref, wsend.at[at], wrecv.at[at], device_id=to, device_id_type=MESH)

    def x_base(k):
        return (z_places[max(k - 1, 0)], 0 if k == 0 else 256)

    def z_base(k):
        return (x_places[max(k - 1, 0)], 256 if k == 0 else 0)

    def x_start(g, k):
        at, base = x_base(k)
        for kind, to in ((0, xp), (1, xm)):
            copy(g, x * 4 + at, base, 256, to, k, kind).start()

    def x_level(g, k, level):
        at, base = x_base(k)
        if level == 1:
            for kind, place, to in ((0, before_x, xp), (1, after_x, xm)):
                shard = place * 4 + at
                copy(g, shard, base, 256, to, k, kind).wait_recv()
                copy(g, shard, base + 128 * kind, 128, to, k, kind + 2).start()
        else:
            shard = across_x * 4 + at
            for kind in range(2):
                copy(g, shard, base + 128 * kind, 128, xp, k, kind + 2).wait_recv()

    def z_start(g, k):
        at, base = z_base(k)
        copy(g, at * 4 + zh, base, 256, near_dev, k + 5, 0).start()

    def z_level(g, k, level):
        at, base = z_base(k)
        mine, theirs = base + 128 * zl, base + 128 * (1 - zl)
        if level == 1:
            copy(g, at * 4 + near_z, base, 256, near_dev, k + 5, 0).wait_recv()
            copy(g, at * 4 + near_z, base, 256, far_dev, k + 5, 1).start()
        elif level == 2:
            copy(g, at * 4 + far_z, base, 256, near_dev, k + 5, 1).wait_recv()
            start = pl.multiple_of(theirs, 128)
            copy(g, at * 4 + far_z, start, 128, near_dev, k + 5, 2).start()
        elif level == 3:
            start = pl.multiple_of(mine, 128)
            copy(g, at * 4 + across_z, start, 128, near_dev, k + 5, 2).wait_recv()
            copy(g, at * 4 + across_z, start, 128, far_dev, k + 5, 3).start()
        else:
            start = pl.multiple_of(theirs, 128)
            copy(g, at * 4 + across_z, start, 128, near_dev, k + 5, 3).wait_recv()

    def begin(g):
        weights_in(g, 0).wait()
        weights_in(g, 1).wait()
        for k in range(2):
            z_start(g, k)
            x_start(g, k)

    def step(g, r):
        events = (
            (("x", 0, 1, "z2", "z3"), ("z", 0, 1, "x2"), ("x", 1, 1), ("z", 1, 1)),
            (("x", 0, 2, "z4"), ("z", 0, 2, "x3"), ("z", 1, 2), ("x", 1, 2), ("z", 2, 1), ("z", 3, 1), ("x", 2, 1)),
            (("z", 0, 3), ("z", 1, 3), ("z", 2, 2), ("z", 3, 2), ("z", 4, 1), ("x", 3, 1), ("x", 2, 2)),
            (("z", 0, 4, "x4"), ("z", 1, 4), ("z", 2, 3), ("z", 3, 3), ("z", 4, 2), ("x", 3, 2)),
            (("x", 4, 1), ("z", 4, 3), ("z", 2, 4), ("z", 3, 4)),
            (("x", 4, 2), ("z", 4, 4)),
        )[r - 1]
        for axis, k, level, *then in events:
            (x_level if axis == "x" else z_level)(g, k, level)
            for name in then:
                (x_start if name[0] == "x" else z_start)(g, int(name[1]))

    def product(g, sx, sz, base):
        return jnp.dot(
            hbuf[sx, :, pl.ds(pl.multiple_of(sz * 512 + base, 256), 256)],
            wbuf[g, sx * 4 + sz, pl.ds(base, 256)],
            preferred_element_type=jnp.float32,
        )

    def multiply(g, tasks):
        sums = acc[...]
        for name in tasks:
            k = int(name[1])
            if name[0] == "x":
                at, base = x_base(k)
                for place in x_places[1:]:
                    sums += product(g, place, at, base)
            else:
                at, base = z_base(k)
                for place in z_places[1:]:
                    sums += product(g, at, place, base)
        acc[...] = sums

    def own(g):
        acc[...] = product(g, x, zh, 0) + product(g, x, zh, 256)

    def kcopy(g, at, kind, unit, to):
        start, size = (2 if kind == 3 else 0), (4 if kind < 2 else 2)
        ref = kv[g].at[pl.ds(unit * 4 + start, size)]
        n = g * 9 + at + kind
        return pltpu.make_async_remote_copy(ref, ref, ksend.at[n], krecv.at[n], device_id=to, device_id_type=MESH)

    def k_send(g, line, kind):
        unit = line * 4 + (y + (0, 0, 3, 1)[kind]) % 4
        at = 4 if isinstance(line, int) else 0
        kcopy(g, at, kind, unit, (yp, ym)[kind % 2]).start()

    def k_wait(g, line, kind):
        unit = line * 4 + (y + (3, 1, 2, 2)[kind]) % 4
        at = 4 if isinstance(line, int) else 0
        kcopy(g, at, kind, unit, yp).wait_recv()

    def cross(g, unit):
        ref = kv[g].at[pl.ds(unit * 4, 4)]
        n = g * 9 + 8
        to = (dp, ctx % 8 + 8)
        return pltpu.make_async_remote_copy(ref, ref, ksend.at[n], krecv.at[n], device_id=to, device_id_type=MESH)

    def kv_begin(g):
        sums = acc[...]
        head = 2 * core + g
        key = sums[:, :D] + bk[head]
        turned = jnp.concatenate([key[:, D // 2:], key[:, : D // 2]], axis=1)
        key = key * cos[...] + turned * sin[...]
        value = sums[:, D:] + bv[head]
        kv[g][pl.ds(m * 4, 4)] = jnp.concatenate([key, value], axis=1).astype(jnp.bfloat16).reshape(4, BLK, 2 * D)

        @pl.when(zl == 0)
        def _():
            cross(g, m).start()
        k_send(g, zl, 0)
        k_send(g, zl, 1)

    def kv_one(g):
        @pl.when(zl == 1)
        def _():
            cross(g, y).wait_recv()
            k_send(g, 0, 0)
            k_send(g, 0, 1)

        for kind in range(2):
            k_wait(g, zl, kind)
            k_send(g, zl, kind + 2)

    def kv_two(g):
        @pl.when(zl == 1)
        def _():
            for kind in range(2):
                k_wait(g, 0, kind)
                k_send(g, 0, kind + 2)

        k_wait(g, zl, 2)
        k_wait(g, zl, 3)

    def kv_three(g):
        @pl.when(zl == 1)
        def _():
            k_wait(g, 0, 2)
            k_wait(g, 0, 3)

    def kv_sent(g):
        for kind in range(4):
            kcopy(g, 0, kind, m, yp).wait_send()

        @pl.when(zl == 1)
        def _():
            for kind in range(4):
                kcopy(g, 4, kind, m, yp).wait_send()

        @pl.when(zl == 0)
        def _():
            cross(g, m).wait_send()

    begin(0)
    for j in (0, 1, 3, 2):
        local, remote = hidden_in(j)
        local.start()
        remote.start()
    q_local.start()
    q_remote.start()
    step(0, 1)
    step(0, 2)
    angles = (m * 512 + lax.broadcasted_iota(jnp.int32, (512, D), 0)).astype(jnp.float32) * frequency[...]
    cos[...] = jnp.cos(angles)
    half = lax.broadcasted_iota(jnp.int32, (512, D), 1) < D // 2
    sin[...] = jnp.where(half, -1.0, 1.0) * jnp.sin(angles)
    step(0, 3)
    begin(1)
    step(0, 4)
    for j in (0, 1, 3, 2):
        hidden_in(j)[0].wait()
        hidden_landed(j).wait_recv()
    own(0)
    multiply(0, ("x0", "x1", "z0", "z1"))
    step(1, 1)
    step(0, 5)
    multiply(0, ("x2", "x3", "z2", "z3"))
    step(1, 2)
    step(0, 6)
    multiply(0, ("x4", "z4"))
    kv_begin(0)
    step(1, 3)
    own(1)
    multiply(1, ("x0", "x1"))
    kv_one(0)
    step(1, 4)
    multiply(1, ("z0", "z1"))
    kv_two(0)
    step(1, 5)
    multiply(1, ("x2", "x3", "z2", "z3"))
    kv_three(0)

    q_local.wait()
    others = pl.ds(pl.multiple_of((1 - core) * 256, 256), 256)
    pltpu.make_async_remote_copy(
        q.at[:, pl.ds(0, 2048)], q2.at[others], hsend.at[4], hrecv.at[4], device_id=sib, device_id_type=MESH).wait_recv()

    pairs = jnp.minimum(m * 4 + 3, 2 * MOST - 1) // 2
    row = lax.broadcasted_iota(jnp.int32, (BLK, 2 * BLK), 0)
    col = lax.broadcasted_iota(jnp.int32, (BLK, 2 * BLK), 1)

    def block_of(i):
        return (i + 2 * (1 - core)) % 4

    def stage(done, ahead):
        order = lambda tile: (tile[0] * 4 + tile[1]) % 2
        if done is not None:
            g_done, b_done, top_ref, s_done = done[0], block_of(done[1]), peaks[order(done)], scores[order(done)]
            top_ref[...] = jnp.broadcast_to(jnp.max(top_ref[...], axis=1, keepdims=True), top_ref.shape)
            total[...] = jnp.zeros_like(total)
            weighted[...] = jnp.zeros_like(weighted)
        if ahead is not None:
            g_ahead, b_ahead, peak_ref, s_ahead = ahead[0], block_of(ahead[1]), peaks[order(ahead)], scores[order(ahead)]
            peak_ref[...] = jnp.full_like(peak_ref, -BIG)
            q_rows = pl.ds(pl.multiple_of(b_ahead * BLK, BLK), BLK)

        def places(b, c, last):
            if last:
                return slots[b, 24], m * 4 + b, 0.0
            return slots[b, 2 * c], slots[b, 2 * c + 1], biases[b, c]

        def two(c0, ends):
            for j in range(8):
                rows = pl.ds(j * BLK, BLK)
                best, share, mixed = None, 0.0, 0.0
                for u in range(2):
                    c, last = c0 + u, ends and u == 1
                    if ahead is not None:
                        first, second, less = places(b_ahead, c, last)
                        keys = jnp.concatenate([kv[g_ahead][first, :, :D], kv[g_ahead][second, :, :D]], axis=0)
                        s = lax.dot_general(
                            q2[q_rows, g_ahead * 1024 + j * D:g_ahead * 1024 + (j + 1) * D], keys,
                            (((1,), (1,)), ((), ())), preferred_element_type=jnp.float32) * SCALE
                        if last:
                            least = jnp.where(col < BLK, slots[b_ahead, 25], col - BLK)
                            s = jnp.where(row >= least, s, -BIG)
                        s_ahead[c, rows] = s
                        here = jnp.maximum(s[:, :BLK], s[:, BLK:])
                        if not last:
                            here = here - less
                        best = here if best is None else jnp.maximum(best, here)
                    if done is not None:
                        first, second, less = places(b_done, c, last)
                        values = jnp.concatenate([kv[g_done][first, :, D:], kv[g_done][second, :, D:]], axis=0)
                        top = top_ref[rows] if last else top_ref[rows] + less
                        left = jnp.exp2(s_done[c, rows, :BLK] - top)
                        right = jnp.exp2(s_done[c, rows, BLK:] - top)
                        share += left + right
                        weights = jnp.concatenate([left, right], axis=1).astype(jnp.bfloat16)
                        mixed += jnp.dot(weights, values, preferred_element_type=jnp.float32)
                if ahead is not None:
                    peak_ref[rows] = jnp.maximum(peak_ref[rows], best)
                if done is not None:
                    total[rows] += share
                    weighted[rows] += mixed

        def main(c, carry):
            two(2 * c, False)
            return carry

        lax.fori_loop(0, (pairs - 1) // 2, main, 0)
        two(pairs - 1, True)
        if done is not None:
            at = done[0] * 4 + done[1]
            for j in range(8):
                rows = pl.ds(j * BLK, BLK)
                tiles[at, :, j * D:(j + 1) * D] = (
                    weighted[rows] / jnp.sum(total[rows], axis=1, keepdims=True)).astype(jnp.bfloat16)
            leaving(*done).start()

    def leaving(g, i):
        cols = pl.ds(pl.multiple_of(core * 2048 + g * 1024, 1024), 1024)
        src, dst = tiles.at[g * 4 + i], out.at[(i % 2) * BLK:(i % 2 + 1) * BLK, cols]
        if i < 2:
            return pltpu.make_async_remote_copy(
                src, dst, osend.at[g * 2 + i], orecv.at[g * 2 + i], device_id=sib, device_id_type=MESH)
        return pltpu.make_async_copy(src, dst, lsem.at[9 + g * 2 + i - 2])

    def coming(g, i):
        cols = pl.ds(pl.multiple_of((1 - core) * 2048 + g * 1024, 1024), 1024)
        return pltpu.make_async_remote_copy(
            tiles.at[g * 4 + i], out.at[i * BLK:(i + 1) * BLK, cols], osend.at[g * 2 + i], orecv.at[g * 2 + i],
            device_id=sib, device_id_type=MESH)

    step(1, 6)
    multiply(1, ("x4", "z4"))
    kv_begin(1)
    stage(None, (0, 0))
    stage((0, 0), (0, 1))
    kv_one(1)
    stage((0, 1), (0, 2))
    kv_two(1)
    stage((0, 2), (0, 3))
    kv_three(1)
    stage((0, 3), (1, 0))
    for i in range(3):
        stage((1, i), (1, i + 1))
    stage((1, 3), None)

    def drain(at, carry):
        for kind in range(4):
            n = at * 4 + kind
            rows = pl.ds(0, 256 if kind < 2 else 128)
            ref = wbuf.at[0, 0, rows]
            pltpu.make_async_remote_copy(
                ref, ref, wsend.at[n], wrecv.at[n], device_id=xp, device_id_type=MESH).wait_send()
        return carry

    lax.fori_loop(0, 20, drain, 0)
    for g in range(2):
        kv_sent(g)
    for j in range(4):
        hidden_in(j)[1].wait_send()
    q_remote.wait_send()
    for g in range(2):
        for i in range(2):
            leaving(g, i).wait_send()
            coming(g, i).wait_recv()
            leaving(g, i + 2).wait()


def attended(slots, biases, hid, q, wk, wv, bk, bv, frequency):
    vmem, anywhere = pl.BlockSpec(memory_space=pltpu.VMEM), pl.BlockSpec(memory_space=pl.ANY)
    smem = pl.BlockSpec(memory_space=pltpu.SMEM)
    bf16, f32, dma = jnp.bfloat16, jnp.float32, pltpu.SemaphoreType.DMA
    return pl.pallas_call(
        whole_kernel,
        out_shape=jax.ShapeDtypeStruct((256, 4096), bf16),
        in_specs=[smem] * 2 + [anywhere] * 4 + [vmem] * 3,
        out_specs=anywhere,
        scratch_shapes=[
            pltpu.VMEM((512, D), f32),
            pltpu.VMEM((512, D), f32),
            pltpu.VMEM((4, 512, 2048), bf16),
            pltpu.VMEM((2, 16, 512, 256), bf16),
            pltpu.VMEM((512, 256), f32),
            pltpu.VMEM((NBLK, BLK, 2 * D), bf16),
            pltpu.VMEM((NBLK, BLK, 2 * D), bf16),
            pltpu.VMEM((512, 2048), bf16),
            pltpu.VMEM((MOST, 8 * BLK, 2 * BLK), f32),
            pltpu.VMEM((MOST, 8 * BLK, 2 * BLK), f32),
            pltpu.VMEM((8 * BLK, BLK), f32),
            pltpu.VMEM((8 * BLK, BLK), f32),
            pltpu.VMEM((8 * BLK, BLK), f32),
            pltpu.VMEM((8 * BLK, D), f32),
            pltpu.VMEM((8, BLK, 8 * D), bf16),
            dma((13,)), dma((5,)), dma((5,)), dma((80,)), dma((80,)), dma((18,)), dma((18,)), dma((4,)), dma((4,)),
        ],
        compiler_params=pltpu.CompilerParams(collective_id=0, has_side_effects=True, vmem_limit_bytes=VMEM_LIMIT),
        name="attended",
    )(slots, biases, hid, q, wk, wv, bk, bv, frequency)


def block_table(segs, first):
    t = first + jnp.arange(4, dtype=jnp.int32)
    at = jnp.arange(NBLK, dtype=jnp.int32)
    before = at[None, :] < t[:, None]
    mine = lax.dynamic_slice_in_dim(segs, first, 4)
    premise = jnp.sum(before & (segs == 0)[None, :], axis=1, dtype=jnp.int32)
    own = jnp.sum(before & (segs[None, :] == mine[:, None]) & (segs != 0)[None, :], axis=1, dtype=jnp.int32)
    seen = premise + own

    def block(j):
        return jnp.minimum(jnp.where(j < premise[:, None], j, j - seen[:, None] + t[:, None]), t[:, None])

    j = jnp.arange(2 * MOST, dtype=jnp.int32)[None, :]
    extra = block(jnp.maximum(seen - 1, 0)[:, None])
    from_row = jnp.where(seen % 2 == 1, -1, BLK)[:, None]
    pairs = jnp.arange(MOST, dtype=jnp.int32)[None, :]
    biases = jnp.where(2 * pairs + 1 < seen[:, None], 0.0, BIG).astype(jnp.float32)
    return jnp.concatenate([block(j), extra, from_row], axis=1).astype(jnp.int32), biases


def body(hidden_in, queries, wk, wv, bk, bv, segs):
    chip = lax.axis_index("ctx") // 2
    frequency = ROPE_BASE ** (-(jnp.arange(D // 2, dtype=jnp.float32) * 2.0 / D))
    frequency = jnp.concatenate([frequency, frequency])[None]
    slots, biases = block_table(segs[0], chip * 4)
    return attended(
        slots, biases, hidden_in[0], queries[0], wk, wv, bk.reshape(4, 1, D), bv.reshape(4, 1, D), frequency)[None]


def solution(mesh):
    placed = (P("dp", "ctx", None), P("dp", "ctx", None), P("dp", None), P("dp", None), P(), P(), P("dp", None))
    return jax.shard_map(body, mesh=mesh, in_specs=placed, out_specs=P("dp", "ctx", None), check_vma=False)
```
